32 devices in a mesh: local: 4 (over y, x), strided: 4 (over z), rep: 2 (over core).
Axes of the slice: x: 2, y: 2, z: 4, core: 2. Of those that a mesh axis runs over, the one named last changes fastest.
Arguments:
- tokens: bfloat16 [2, 512, 1440], P('rep', ('local', 'strided')), may hold values from -6 to 6
- experts: int32 [2, 512, 4], P('rep', ('local', 'strided')), may hold values from 0 to 15, as said below
- slots: int32 [2, 512, 4], P('rep', ('local', 'strided')), may hold values from -1 to 127, as said below
- route_weight: float32 [2, 512, 4], P('rep', ('local', 'strided')), may hold values from 0.05 to 0.8
- out_grad: bfloat16 [2, 512, 1440], P('rep', ('local', 'strided')), may hold values from -1.5 to 1.5
- w_gate: bfloat16 [16, 1440, 1440], P(('local', 'strided'), None, 'rep'), may hold values from -0.15625 to 0.15625
- w_up: bfloat16 [16, 1440, 1440], P(('local', 'strided'), None, 'rep'), may hold values from -0.15625 to 0.15625
- w_down: bfloat16 [16, 1440, 1440], P(('local', 'strided'), 'rep'), may hold values from -0.15625 to 0.15625
Outputs:
- mixed: bfloat16 [2, 512, 1440], P('rep', ('local', 'strided'))
- token_grad: bfloat16 [2, 512, 1440], P('rep', ('local', 'strided'))
- weight_grad: float32 [2, 512, 4], P('rep', ('local', 'strided'))
- gate_grad: bfloat16 [16, 1440, 1440], P(('local', 'strided'), None, 'rep')
- up_grad: bfloat16 [16, 1440, 1440], P(('local', 'strided'), None, 'rep')
- down_grad: bfloat16 [16, 1440, 1440], P(('local', 'strided'), 'rep')
The draws below stay inside these ranges and needn't reach their ends.
Inputs may be any that keep to these rules, and one draw needn't show every extreme that they name: Each row names 4 different experts. The 32 rows of one device of a replica name each expert at most 16 times, and some expert exactly 16 times. slots[r, t, k] is the number of pairs of replica r that come before (t, k) in token order and name the same expert, where that number is below 128; otherwise it is -1 and the pair is dropped.
All inputs are finite; a program needn't handle non-finite values.
Results may differ from the reference program's by a relative error of at most 0.0064.
Values may be sent and summed in bfloat16 or wider, within the bound.
A program may use at most 192 MiB of HBM per device.

```python
import math
import jax
import jax.numpy as jnp
from jax import lax

D = 1440
FF = 1440
TOP = 4
TOK_DEV = 32
REPLICAS = 2
EXPERTS = 16
TOKENS = 512
CAP = 128
MOST = 16


def routing_tables(key):
    base_key = jax.random.fold_in(key, 11)
    block_count = REPLICAS * EXPERTS
    pair_total = TOK_DEV * TOP

    def one_block(block_key):
        perm_key, share_key = jax.random.split(block_key)
        expert_order = jax.random.permutation(perm_key, EXPERTS).astype(jnp.int32)
        shares = jax.random.randint(share_key, (EXPERTS // 2,), 0, MOST + 1).astype(jnp.int32)
        shares = shares.at[0].set(MOST)
        counts = jnp.stack([shares, MOST - shares], axis=1).reshape(-1)
        run_ends = jnp.cumsum(counts)
        positions = jnp.arange(pair_total, dtype=jnp.int32)
        run_index = jnp.searchsorted(run_ends, positions, side='right')
        listed = expert_order[run_index]
        return listed.reshape(TOP, TOK_DEV).T
    block_keys = jax.random.split(base_key, block_count)
    chosen = jax.vmap(one_block)(block_keys).reshape(REPLICAS, TOKENS, TOP).astype(jnp.int32)

    def slots_of(replica_ids):
        flat_ids = replica_ids.reshape(-1)
        onehot = (flat_ids[:, None] == jnp.arange(EXPERTS, dtype=jnp.int32)[None, :]).astype(jnp.int32)
        earlier = jnp.sum((jnp.cumsum(onehot, axis=0) - onehot) * onehot, axis=1)
        return jnp.where(earlier < CAP, earlier, -1).reshape(TOKENS, TOP)
    slot_table = jax.vmap(slots_of)(chosen).astype(jnp.int32)
    return (chosen, slot_table)


def draw_experts(key, part):
    return routing_tables(key)[0]


def draw_slots(key, part):
    return routing_tables(key)[1]


def level_of(key, extent, cuts, smallest, largest):
    def one(axis_at, blocks):
        draws = jax.random.uniform(jax.random.fold_in(jax.random.fold_in(key, 6), axis_at), (blocks,), jnp.float32, smallest / len(cuts), largest / len(cuts))
        return jnp.repeat(jnp.exp(draws), extent[axis_at] // blocks).reshape((-1,) + (1,) * (len(extent) - axis_at - 1))

    loudness = one(*cuts[0])
    for cut in cuts[1:]:
        loudness = loudness * one(*cut)
    return loudness


def bell_draw(rng, dims, deviation, limit, cuts=(), kind=jnp.bfloat16):
    factor_of = level_of(rng, dims, cuts, -0.22, 0.18) if cuts else 1.0
    entries = jax.random.normal(rng, dims, jnp.float32) * deviation * factor_of
    return jnp.minimum(jnp.maximum(entries, -limit), limit).astype(kind)


def setup_inputs(seed: int = 0) -> dict:
    key_of = jax.random.split(jax.random.key(seed), 9)
    return {
        "tokens": bell_draw(key_of[0], (REPLICAS, TOKENS, D), 1.0, 6.0, ((0, 2), (1, 16))),
        "experts": draw_experts(jax.random.fold_in(key_of[8], 71), 0),
        "slots": draw_slots(jax.random.fold_in(key_of[8], 71), 0),
        "route_weight": jnp.clip(jnp.exp(math.log(0.8) - 2.7725887 * jax.random.uniform(key_of[3], (REPLICAS, TOKENS, TOP), jnp.float32) ** level_of(key_of[3], (REPLICAS, TOKENS, TOP), ((0, 2), (1, 16)), -0.2, 0.2)), 0.05, 0.8),
        "out_grad": bell_draw(key_of[4], (REPLICAS, TOKENS, D), 0.25, 1.5, ((0, 2), (1, 16))),
        "w_gate": bell_draw(key_of[5], (EXPERTS, D, FF), D ** -0.5, 0.15625, ((0, 16), (2, 2))),
        "w_up": bell_draw(key_of[6], (EXPERTS, D, FF), D ** -0.5, 0.15625, ((0, 16), (2, 2))),
        "w_down": bell_draw(key_of[7], (EXPERTS, FF, D), FF ** -0.5, 0.15625, ((0, 16), (1, 2))),
    }


SWIGLU_ALPHA = 1.702


def swiglu(gate_pre, up_pre):
    return (up_pre + 1.0) * gate_pre * jax.nn.sigmoid(SWIGLU_ALPHA * gate_pre)


def swiglu_grads(grad_hidden, gate_pre, up_pre):
    sigmoid_gate = jax.nn.sigmoid(SWIGLU_ALPHA * gate_pre)
    grad_up = grad_hidden * gate_pre * sigmoid_gate
    slope = sigmoid_gate + SWIGLU_ALPHA * gate_pre * sigmoid_gate * (1.0 - sigmoid_gate)
    grad_gate = grad_hidden * (up_pre + 1.0) * slope
    return grad_gate.astype(jnp.bfloat16), grad_up.astype(jnp.bfloat16)


def contract(left, right, left_dim, right_dim):
    return lax.dot_general(left, right, (((left_dim,), (right_dim,)), ((), ())), preferred_element_type=jnp.float32)


def expert_pass(operands):
    expert_rows, expert_grads, gate_weight, up_weight, down_weight = operands
    gate_pre = contract(expert_rows, gate_weight, 1, 0)
    up_pre = contract(expert_rows, up_weight, 1, 0)
    hidden = swiglu(gate_pre, up_pre).astype(jnp.bfloat16)
    expert_out = contract(hidden, down_weight, 1, 0).astype(jnp.bfloat16)
    grad_hidden = contract(expert_grads, down_weight, 1, 1)
    grad_gate, grad_up = swiglu_grads(grad_hidden, gate_pre, up_pre)
    down_grad = contract(hidden, expert_grads, 0, 0).astype(jnp.bfloat16)
    gate_grad = contract(expert_rows, grad_gate, 0, 0).astype(jnp.bfloat16)
    up_grad = contract(expert_rows, grad_up, 0, 0).astype(jnp.bfloat16)
    rows_grad = (contract(grad_gate, gate_weight, 1, 1) + contract(grad_up, up_weight, 1, 1)).astype(jnp.bfloat16)
    return expert_out, rows_grad, gate_grad, up_grad, down_grad


def reference(tokens, experts, slots, route_weight, out_grad, w_gate, w_up, w_down):
    rep_count, token_count, top_count = experts.shape
    expert_count = w_gate.shape[0]
    capacity = token_count * top_count // expert_count
    model_width = tokens.shape[2]
    kept_mask = (slots >= 0).reshape(rep_count, -1)
    pair_index = jnp.where(slots >= 0, experts * capacity + slots, expert_count * capacity).astype(jnp.int32).reshape(rep_count, -1)
    pair_rows = jnp.broadcast_to(tokens[:, :, None, :], (rep_count, token_count, top_count, model_width)).reshape(rep_count, -1, model_width)
    pair_grads = (route_weight[..., None] * out_grad[:, :, None, :].astype(jnp.float32)).astype(jnp.bfloat16).reshape(rep_count, -1, model_width)

    def place(values, positions):
        return jnp.zeros((expert_count * capacity, model_width), values.dtype).at[positions].set(values, mode="drop")

    def arrange(buffer):
        return buffer.reshape(rep_count, expert_count, capacity, model_width).transpose(1, 0, 2, 3).reshape(expert_count, rep_count * capacity, model_width)

    def unarrange(buffer):
        return buffer.reshape(expert_count, rep_count, capacity, model_width).transpose(1, 0, 2, 3).reshape(rep_count, expert_count * capacity, model_width)

    def collect(buffer, positions, mask):
        picked = buffer[jnp.where(mask, positions, 0)]
        return jnp.where(mask[:, None], picked, jnp.zeros_like(picked))

    dispatched = arrange(jax.vmap(place)(pair_rows, pair_index))
    expert_grads = arrange(jax.vmap(place)(pair_grads, pair_index))
    expert_out, rows_grad, gate_grad, up_grad, down_grad = lax.map(expert_pass, (dispatched, expert_grads, w_gate, w_up, w_down))
    pair_out = jax.vmap(collect)(unarrange(expert_out), pair_index, kept_mask).reshape(rep_count, token_count, top_count, model_width)
    mixed = jnp.sum(route_weight[..., None] * pair_out.astype(jnp.float32), axis=2).astype(jnp.bfloat16)
    weight_grad = jnp.sum(out_grad[:, :, None, :].astype(jnp.float32) * pair_out.astype(jnp.float32), axis=3)
    pair_dx = jax.vmap(collect)(unarrange(rows_grad), pair_index, kept_mask).reshape(rep_count, token_count, top_count, model_width)
    token_grad = jnp.sum(pair_dx.astype(jnp.float32), axis=2).astype(jnp.bfloat16)
    return mixed, token_grad, weight_grad, gate_grad, up_grad, down_grad
```

```python
import functools

import jax
import jax.numpy as jnp
from jax import lax
from jax.experimental import pallas as pl
from jax.experimental.pallas import tpu as pltpu
from jax.sharding import PartitionSpec as P

SWIGLU_ALPHA = 1.702
BF = jnp.bfloat16
F32 = jnp.float32
MESH = pl.DeviceIdType.MESH


def contract(left, right, left_dim, right_dim):
    return lax.dot_general(
        left, right, (((left_dim,), (right_dim,)), ((), ())), preferred_element_type=F32
    )


def xor(index, constant, size):
    result, bit = 0, 1
    while bit < size:
        result = result + bit * lax.rem(lax.div(index, bit) + (constant // bit) % 2, 2)
        bit *= 2
    return result


def three_parts(value):
    high = value.astype(BF).astype(F32)
    middle = (value - high).astype(BF).astype(F32)
    low = (value - high - middle).astype(BF).astype(F32)
    return high, middle, low


def kernel(
    sizes,
    tokens,
    experts,
    slots,
    router,
    out_grad,
    gate_hbm,
    up_hbm,
    down_hbm,
    mixed,
    token_grad,
    weight_grad,
    gate_grad_hbm,
    up_grad_hbm,
    down_grad_hbm,
    w_gate,
    w_up,
    w_down,
    d_gate,
    d_up,
    d_down,
    gathered,
    plane_out,
    plane_in,
    back_out,
    back_in,
    home_out,
    home_in,
    select,
    place,
    rows,
    grads,
    hidden,
    gate_pre,
    up_pre,
    slope_gate,
    slope_up,
    partial,
    other,
    reply,
    w_sem,
    d_sem,
    z_send,
    z_recv,
    p_send,
    p_recv,
    r_send,
    r_recv,
    h_send,
    h_recv,
    c_send,
    c_recv,
):
    S, L, T, TOP, PM, G, R, D, DP, CAP = sizes
    NG, TT, LR = S // G, G * T, L * R
    TB = DP - 128
    OFF = D - TB
    l, s, r = lax.axis_index("local"), lax.axis_index("strided"), lax.axis_index("rep")
    twin = 1 - r
    strided_peers = [xor(s, j, S) for j in range(S)]
    local_peers = [xor(l, j, L) for j in range(L)]
    groups = [xor(lax.div(s, G), j, NG) for j in range(NG)]

    loads = [
        pltpu.make_async_copy(source.at[0], target, w_sem.at[i])
        for i, (source, target) in enumerate(
            ((gate_hbm, w_gate), (up_hbm, w_up), (down_hbm, w_down))
        )
    ]
    for load in loads:
        load.start()

    barrier = pltpu.get_barrier_semaphore()
    for j in range(1, S):
        pl.semaphore_signal(
            barrier, inc=1, device_id=(l, strided_peers[j], r), device_id_type=MESH
        )
    for j in range(1, L):
        pl.semaphore_signal(barrier, inc=1, device_id=(local_peers[j], s, r), device_id_type=MESH)
    pl.semaphore_signal(barrier, inc=1, device_id=(l, s, twin), device_id_type=MESH)

    lane = lax.broadcasted_iota(jnp.int32, (T, 128), 1) - OFF
    gathered[0, s, :, TB:] = jnp.zeros((T, 128), BF)
    gathered[1, s, :, TB:] = jnp.zeros((T, 128), BF)
    gathered[0, s, :, :D] = tokens[0]
    gathered[1, s, :, :D] = out_grad[0]
    tail = gathered[0, s, :, TB:].astype(F32)
    named = experts[0].astype(F32)
    slotted = slots[0].astype(F32) + 1.0
    parts = (named, slotted) + three_parts(router[0])
    for i, part in enumerate(parts):
        for k in range(TOP):
            tail = jnp.where(lane == i * TOP + k, part[:, k : k + 1], tail)
    gathered[0, s, :, TB:] = tail.astype(BF)

    pl.semaphore_wait(barrier, (S - 1) + (L - 1) + 1)

    pending = []

    def send(source, target, send_sem, recv_sem, device):
        copy = pltpu.make_async_remote_copy(
            src_ref=source,
            dst_ref=target,
            send_sem=send_sem,
            recv_sem=recv_sem,
            device_id=device,
            device_id_type=MESH,
        )
        copy.start()
        pending.append(copy)
        return copy

    def arrival(target, send_sem, recv_sem, device):
        return pltpu.make_async_remote_copy(
            src_ref=target,
            dst_ref=target,
            send_sem=send_sem,
            recv_sem=recv_sem,
            device_id=device,
            device_id_type=MESH,
        )

    for kind in range(2):
        for j in range(1, S):
            send(
                gathered.at[kind, s],
                gathered.at[kind, s],
                z_send.at[kind, j],
                z_recv.at[kind, s],
                (l, strided_peers[j], r),
            )

    def await_strided(kind, buffer, sends, recvs, j):
        peer = strided_peers[j]
        arrival(
            buffer.at[kind, peer], sends.at[kind, j], recvs.at[kind, peer], (l, peer, r)
        ).wait_recv()

    def await_local(kind, buffer, sends, recvs, group, j):
        peer = local_peers[j]
        arrival(
            buffer.at[kind, group, peer],
            sends.at[kind, group, j],
            recvs.at[kind, group, peer],
            (peer, s, r),
        ).wait_recv()

    def send_local(kind, outgoing, incoming, sends, recvs, group):
        for j in range(1, L):
            send(
                outgoing.at[kind, group, local_peers[j]],
                incoming.at[kind, group, l],
                sends.at[kind, group, j],
                recvs.at[kind, group, l],
                (local_peers[j], s, r),
            )
        incoming[kind, group, l] = outgoing[kind, group, l]

    column = lax.broadcasted_iota(jnp.int32, (TT, LR), 1)
    token = lax.broadcasted_iota(jnp.int32, (TT, LR), 0)
    wanted = (lax.div(column, R) * S + s).astype(F32)
    same_source = lax.div(token, T) == lax.div(lax.rem(column, R), PM)
    rank_wanted = lax.rem(column, PM).astype(F32)
    below = (
        lax.broadcasted_iota(jnp.int32, (TT, TT), 1) < lax.broadcasted_iota(jnp.int32, (TT, TT), 0)
    ).astype(F32).astype(BF)
    group_lane = lax.broadcasted_iota(jnp.int32, (TT, 128), 1) - OFF
    row_lane = lax.broadcasted_iota(jnp.int32, (LR, 128), 1) - OFF

    for jg in range(NG):
        group = groups[jg]
        for j in range(max(1, jg * G), (jg + 1) * G):
            await_strided(0, gathered, z_send, z_recv, j)
        block = gathered[0, pl.ds(group * G, G)].reshape(TT, DP)
        route = block[:, TB:].astype(F32)

        def lane_of(i, k):
            return route[:, OFF + i * TOP + k : OFF + i * TOP + k + 1]

        hits = []
        for k in range(TOP):
            hit = (lane_of(0, k) == wanted) & (lane_of(1, k) > 0.0) & same_source
            hits.append(hit.astype(F32))
        hit_any = sum(hits)
        rank = contract(below, hit_any.astype(BF), 1, 0)
        picked = jnp.where(rank == rank_wanted, hit_any, 0.0)
        picked_bf = picked.astype(BF)
        select[group] = picked_bf
        moved = contract(picked_bf, block, 0, 0)
        info = jnp.zeros((LR, 128), F32)
        for k in range(TOP):
            values = jnp.where(group_lane == 0, lane_of(1, k), 0.0)
            values = jnp.where(group_lane == 1, float(k), values)
            for i in range(3):
                values = jnp.where(group_lane == 2 + i, lane_of(2 + i, k), values)
            info = info + contract((picked * hits[k]).astype(BF), values.astype(BF), 0, 0)
        plane_out[0, group, :, :, :TB] = moved[:, :TB].astype(BF).reshape(L, R, TB)
        plane_out[0, group, :, :, TB:] = (
            jnp.where(row_lane < 0, moved[:, TB:], info).astype(BF).reshape(L, R, 128)
        )
        send_local(0, plane_out, plane_in, p_send, p_recv, group)

    for jg in range(NG):
        group = groups[jg]
        for j in range(max(1, jg * G), (jg + 1) * G):
            await_strided(1, gathered, z_send, z_recv, j)
        block = gathered[1, pl.ds(group * G, G)].reshape(TT, DP)
        moved = contract(select[group], block, 0, 0)
        plane_out[1, group] = moved.astype(BF).reshape(L, R, DP)
        send_local(1, plane_out, plane_in, p_send, p_recv, group)

    def swap(index, source, target):
        copy = send(source, target, c_send.at[index], c_recv.at[index], (l, s, twin))
        return copy

    def await_plane(kind):
        for jg in range(NG):
            for j in range(1, L):
                await_local(kind, plane_in, p_send, p_recv, groups[jg], j)

    await_plane(0)
    received = plane_in[0].reshape(NG * LR, DP)
    slot_of = received[:, TB:].astype(F32)[:, OFF : OFF + 1]
    slot_lane = lax.broadcasted_iota(jnp.int32, (NG * LR, CAP), 1).astype(F32) + 1.0
    place[...] = (slot_of == slot_lane).astype(F32).astype(BF)
    rows[0, r] = contract(place[...], received, 0, 0).astype(BF)
    swap(0, rows.at[0, r], rows.at[0, r])
    for load in loads:
        load.wait()
    arrival(rows.at[0, twin], c_send.at[0], c_recv.at[0], (l, s, twin)).wait_recv()

    x = rows[0].reshape(2 * CAP, DP)[:, :D]
    gate = contract(x, w_gate[...], 1, 0)
    gate_pre[...] = gate
    up = contract(x, w_up[...], 1, 0)
    up_pre[...] = up
    hidden[...] = ((up + 1.0) * gate * jax.nn.sigmoid(SWIGLU_ALPHA * gate)).astype(BF)
    partial[0] = contract(hidden[...], w_down[...], 1, 0).reshape(2, CAP, D)
    swap(1, partial.at[0, twin], other.at[0])

    def weight_of(tail):
        return (
            tail[:, OFF + 2 : OFF + 3] + tail[:, OFF + 3 : OFF + 4] + tail[:, OFF + 4 : OFF + 5]
        )

    weight_rows = weight_of(rows[0].reshape(2 * CAP, DP)[:, TB:].astype(F32))
    own_tail = rows[0, r, :, TB:].astype(F32)
    arrival(other.at[0], c_send.at[1], c_recv.at[1], (l, s, twin)).wait_recv()
    out = partial[0, r] + other[0]
    reply[0, :, TB:] = jnp.zeros((CAP, 128), BF)
    reply[0, :, :D] = (weight_of(own_tail) * out).astype(BF)
    back_out[0] = contract(place[...], reply[0], 1, 0).astype(BF).reshape(NG, L, R, DP)
    for jg in reversed(range(NG)):
        send_local(0, back_out, back_in, r_send, r_recv, groups[jg])

    await_plane(1)
    rows[1, r] = contract(place[...], plane_in[1].reshape(NG * LR, DP), 0, 0).astype(BF)
    swap(2, rows.at[1, r], rows.at[1, r])
    own_grads = rows[1, r, :, :D].astype(F32)
    router_grad = jnp.sum(own_grads * out, axis=1, keepdims=True)
    slot_tail = lax.broadcasted_iota(jnp.int32, (CAP, 128), 1).astype(F32) - float(OFF)
    which = own_tail[:, OFF + 1 : OFF + 2]
    reply_tail = jnp.zeros((CAP, 128), F32)
    for i, part in enumerate(three_parts(router_grad)):
        reply_tail = jnp.where(slot_tail == which + float(i * TOP), part, reply_tail)
    arrival(rows.at[1, twin], c_send.at[2], c_recv.at[2], (l, s, twin)).wait_recv()
    grads[...] = (weight_rows * rows[1].reshape(2 * CAP, DP)[:, :D].astype(F32)).astype(BF)
    grad_hidden = contract(grads[...], w_down[...], 1, 1)
    gate = gate_pre[...]
    sig = jax.nn.sigmoid(SWIGLU_ALPHA * gate)
    slope_up[...] = (grad_hidden * gate * sig).astype(BF)
    slope = sig + SWIGLU_ALPHA * gate * sig * (1.0 - sig)
    slope_gate[...] = (grad_hidden * (up_pre[...] + 1.0) * slope).astype(BF)
    partial[1] = (
        contract(slope_gate[...], w_gate[...], 1, 1) + contract(slope_up[...], w_up[...], 1, 1)
    ).reshape(2, CAP, D)
    swap(3, partial.at[1, twin], other.at[1])

    stores = []

    def store(index, source, target):
        copy = pltpu.make_async_copy(source, target.at[0], d_sem.at[index])
        copy.start()
        stores.append(copy)

    d_down[...] = contract(hidden[...], grads[...], 0, 0).astype(BF)
    store(2, d_down, down_grad_hbm)

    arrival(other.at[1], c_send.at[3], c_recv.at[3], (l, s, twin)).wait_recv()
    reply[1, :, TB:] = jnp.zeros((CAP, 128), BF)
    reply[1, :, :D] = (partial[1, r] + other[1]).astype(BF)
    reply[1, :, TB:] = jnp.where(
        slot_tail < 0.0, reply[1, :, TB:].astype(F32), reply_tail
    ).astype(BF)
    back_out[1] = contract(place[...], reply[1], 1, 0).astype(BF).reshape(NG, L, R, DP)
    for jg in reversed(range(NG)):
        send_local(1, back_out, back_in, r_send, r_recv, groups[jg])

    def send_home(kind):
        for jg in reversed(range(NG)):
            group = groups[jg]
            for j in range(1, L):
                await_local(kind, back_in, r_send, r_recv, group, j)
            total = contract(select[group], back_in[kind, group].reshape(LR, DP), 1, 0)
            home_out[kind, pl.ds(group * G, G)] = total.astype(BF).reshape(G, T, DP)
            for j in range(jg * G, (jg + 1) * G):
                peer = strided_peers[j]
                if j == 0:
                    home_in[kind, s] = home_out[kind, s]
                else:
                    send(
                        home_out.at[kind, peer],
                        home_in.at[kind, s],
                        h_send.at[kind, j],
                        h_recv.at[kind, s],
                        (l, peer, r),
                    )

    send_home(0)
    x = rows[0].reshape(2 * CAP, DP)[:, :D]
    d_gate[...] = contract(x, slope_gate[...], 0, 0).astype(BF)
    store(0, d_gate, gate_grad_hbm)
    d_up[...] = contract(x, slope_up[...], 0, 0).astype(BF)
    store(1, d_up, up_grad_hbm)
    send_home(1)

    def collect(kind):
        for j in range(1, S):
            await_strided(kind, home_in, h_send, h_recv, j)
        total = home_in[kind, 0].astype(F32)
        for j in range(1, S):
            total = total + home_in[kind, j].astype(F32)
        return total

    mixed[0] = collect(0)[:, :D].astype(BF)
    total = collect(1)
    token_grad[0] = total[:, :D].astype(BF)
    tail = total[:, TB:]
    weight_grad[0] = tail[:, OFF : OFF + TOP] + (
        tail[:, OFF + TOP : OFF + 2 * TOP] + tail[:, OFF + 2 * TOP : OFF + 3 * TOP]
    )
    for copy in stores:
        copy.wait()
    for copy in pending:
        copy.wait_send()


def local(tokens, experts, slots, route_weight, out_grad, w_gate, w_up, w_down):
    L, S = lax.axis_size("local"), lax.axis_size("strided")
    T, D = tokens.shape[1:]
    TOP = experts.shape[2]
    F = w_gate.shape[2]
    CAP = T * TOP
    PM = 2 * CAP // (L * S)
    G = max(1, 16 // PM)
    R = G * PM
    NG, TT, LR = S // G, G * T, L * R
    DP = -(-(D + 5 * TOP) // 128) * 128
    sizes = (S, L, T, TOP, PM, G, R, D, DP, CAP)
    vmem = pl.BlockSpec(memory_space=pltpu.VMEM)
    anywhere = pl.BlockSpec(memory_space=pl.ANY)
    dma = pltpu.SemaphoreType.DMA
    return pl.pallas_call(
        functools.partial(kernel, sizes),
        out_shape=(
            jax.ShapeDtypeStruct((1, T, D), BF),
            jax.ShapeDtypeStruct((1, T, D), BF),
            jax.ShapeDtypeStruct((1, T, TOP), F32),
            jax.ShapeDtypeStruct((1, D, F), BF),
            jax.ShapeDtypeStruct((1, D, F), BF),
            jax.ShapeDtypeStruct((1, F, D), BF),
        ),
        in_specs=[vmem] * 5 + [anywhere] * 3,
        out_specs=[vmem] * 3 + [anywhere] * 3,
        scratch_shapes=[
            pltpu.VMEM((D, F), BF),
            pltpu.VMEM((D, F), BF),
            pltpu.VMEM((F, D), BF),
            pltpu.VMEM((D, F), BF),
            pltpu.VMEM((D, F), BF),
            pltpu.VMEM((F, D), BF),
            pltpu.VMEM((2, S, T, DP), BF),
            pltpu.VMEM((2, NG, L, R, DP), BF),
            pltpu.VMEM((2, NG, L, R, DP), BF),
            pltpu.VMEM((2, NG, L, R, DP), BF),
            pltpu.VMEM((2, NG, L, R, DP), BF),
            pltpu.VMEM((2, S, T, DP), BF),
            pltpu.VMEM((2, S, T, DP), BF),
            pltpu.VMEM((NG, TT, LR), BF),
            pltpu.VMEM((NG * LR, CAP), BF),
            pltpu.VMEM((2, 2, CAP, DP), BF),
            pltpu.VMEM((2 * CAP, D), BF),
            pltpu.VMEM((2 * CAP, F), BF),
            pltpu.VMEM((2 * CAP, F), F32),
            pltpu.VMEM((2 * CAP, F), F32),
            pltpu.VMEM((2 * CAP, F), BF),
            pltpu.VMEM((2 * CAP, F), BF),
            pltpu.VMEM((2, 2, CAP, D), F32),
            pltpu.VMEM((2, CAP, D), F32),
            pltpu.VMEM((2, CAP, DP), BF),
            dma((3,)),
            dma((3,)),
            dma((2, S)),
            dma((2, S)),
            dma((2, NG, L)),
            dma((2, NG, L)),
            dma((2, NG, L)),
            dma((2, NG, L)),
            dma((2, S)),
            dma((2, S)),
            dma((4,)),
            dma((4,)),
        ],
        compiler_params=pltpu.CompilerParams(
            collective_id=0, has_side_effects=True, vmem_limit_bytes=58 * 1024 * 1024
        ),
        cost_estimate=pl.CostEstimate(
            flops=18 * 2 * CAP * D * F, bytes_accessed=12 * D * F, transcendentals=4 * CAP * F
        ),
        name="moe_layer",
    )(tokens, experts, slots, route_weight, out_grad, w_gate, w_up, w_down)


def solution(mesh):
    pairs = P("rep", ("local", "strided"), None)
    split_last = P(("local", "strided"), None, "rep")
    split_middle = P(("local", "strided"), "rep", None)
    return jax.shard_map(
        local,
        mesh=mesh,
        in_specs=(pairs,) * 5 + (split_last, split_last, split_middle),
        out_specs=(pairs,) * 3 + (split_last, split_last, split_middle),
        check_vma=False,
    )
```

```python
import functools

import jax
import jax.numpy as jnp
from jax import lax
from jax.experimental import pallas as pl
from jax.experimental.pallas import tpu as pltpu
from jax.sharding import PartitionSpec as P

SWIGLU_ALPHA = 1.702
BF = jnp.bfloat16
F32 = jnp.float32
MESH = pl.DeviceIdType.MESH


def contract(left, right, left_dim, right_dim):
    return lax.dot_general(
        left, right, (((left_dim,), (right_dim,)), ((), ())), preferred_element_type=F32
    )


def xor(index, constant, size):
    result, bit = 0, 1
    while bit < size:
        result = result + bit * lax.rem(lax.div(index, bit) + (constant // bit) % 2, 2)
        bit *= 2
    return result


def three_parts(value):
    high = value.astype(BF).astype(F32)
    middle = (value - high).astype(BF).astype(F32)
    low = (value - high - middle).astype(BF).astype(F32)
    return high, middle, low


def kernel(
    sizes,
    tokens,
    experts,
    slots,
    router,
    out_grad,
    gate_hbm,
    up_hbm,
    down_hbm,
    mixed,
    token_grad,
    weight_grad,
    rows_hbm,
    grads_hbm,
    hidden_hbm,
    slope_gate_hbm,
    slope_up_hbm,
    w_gate,
    w_up,
    w_down,
    routing,
    gathered,
    plane_out,
    plane_in,
    back_out,
    back_in,
    home_out,
    home_in,
    select,
    place,
    rows,
    grads,
    hidden,
    gate_pre,
    up_pre,
    slope_gate,
    slope_up,
    partial,
    other,
    reply,
    w_sem,
    d_sem,
    z_send,
    z_recv,
    p_send,
    p_recv,
    r_send,
    r_recv,
    h_send,
    h_recv,
    c_send,
    c_recv,
):
    S, L, T, TOP, PM, G, R, D, DP, CAP = sizes
    NG, TT, LR = S // G, G * T, L * R
    TB = DP - 128
    OFF = D - TB
    l, s, r = lax.axis_index("local"), lax.axis_index("strided"), lax.axis_index("rep")
    twin = 1 - r
    strided_peers = [xor(s, j, S) for j in range(S)]
    local_peers = [xor(l, j, L) for j in range(L)]
    groups = [xor(lax.div(s, G), j, NG) for j in range(NG)]

    loads = [
        pltpu.make_async_copy(source.at[0], target, w_sem.at[i])
        for i, (source, target) in enumerate(
            ((gate_hbm, w_gate), (up_hbm, w_up), (down_hbm, w_down))
        )
    ]
    for load in loads:
        load.start()

    barrier = pltpu.get_barrier_semaphore()
    for j in range(1, S):
        pl.semaphore_signal(
            barrier, inc=1, device_id=(l, strided_peers[j], r), device_id_type=MESH
        )
    for j in range(1, L):
        pl.semaphore_signal(barrier, inc=1, device_id=(local_peers[j], s, r), device_id_type=MESH)
    pl.semaphore_signal(barrier, inc=1, device_id=(l, s, twin), device_id_type=MESH)

    lane = lax.broadcasted_iota(jnp.int32, (T, 128), 1) - OFF
    gathered[0, s, :, TB:] = jnp.zeros((T, 128), BF)
    gathered[1, s, :, TB:] = jnp.zeros((T, 128), BF)
    gathered[0, s, :, :D] = tokens[0]
    gathered[1, s, :, :D] = out_grad[0]
    routing[...] = jnp.zeros(routing.shape, F32)
    parts = (experts[0].astype(F32), slots[0].astype(F32) + 1.0) + three_parts(router[0])
    for i, part in enumerate(parts):
        routing[i * 16 : i * 16 + TOP, :] = part
    line = lax.broadcasted_iota(jnp.int32, (80, 128), 0)
    spot = lax.broadcasted_iota(jnp.int32, (80, 128), 1) - OFF
    spread = (lax.rem(line, 16) < TOP) & (spot == lax.div(line, 16) * TOP + lax.rem(line, 16))
    info = contract(routing[...].astype(BF), spread.astype(F32).astype(BF), 0, 0)
    tail = gathered[0, s, :, TB:].astype(F32)
    gathered[0, s, :, TB:] = jnp.where(lane < 0, tail, info).astype(BF)

    pl.semaphore_wait(barrier, (S - 1) + (L - 1) + 1)

    pending = []

    def send(source, target, send_sem, recv_sem, device):
        copy = pltpu.make_async_remote_copy(
            src_ref=source,
            dst_ref=target,
            send_sem=send_sem,
            recv_sem=recv_sem,
            device_id=device,
            device_id_type=MESH,
        )
        copy.start()
        pending.append(copy)
        return copy

    def arrival(target, send_sem, recv_sem, device):
        return pltpu.make_async_remote_copy(
            src_ref=target,
            dst_ref=target,
            send_sem=send_sem,
            recv_sem=recv_sem,
            device_id=device,
            device_id_type=MESH,
        )

    def send_strided(kind, j):
        send(
            gathered.at[kind, s],
            gathered.at[kind, s],
            z_send.at[kind, j],
            z_recv.at[kind, s],
            (l, strided_peers[j], r),
        )

    for j in range(1, S):
        send_strided(0, j)

    def await_strided(kind, buffer, sends, recvs, j):
        peer = strided_peers[j]
        arrival(
            buffer.at[kind, peer], sends.at[kind, j], recvs.at[kind, peer], (l, peer, r)
        ).wait_recv()

    def await_local(kind, buffer, sends, recvs, group, j):
        peer = local_peers[j]
        arrival(
            buffer.at[kind, group, peer],
            sends.at[kind, group, j],
            recvs.at[kind, group, peer],
            (peer, s, r),
        ).wait_recv()

    def send_local(kind, outgoing, incoming, sends, recvs, group):
        for j in range(1, L):
            send(
                outgoing.at[kind, group, local_peers[j]],
                incoming.at[kind, group, l],
                sends.at[kind, group, j],
                recvs.at[kind, group, l],
                (local_peers[j], s, r),
            )
        incoming[kind, group, l] = outgoing[kind, group, l]

    column = lax.broadcasted_iota(jnp.int32, (TT, LR), 1)
    token = lax.broadcasted_iota(jnp.int32, (TT, LR), 0)
    wanted = (lax.div(column, R) * S + s).astype(F32)
    same_source = lax.div(token, T) == lax.div(lax.rem(column, R), PM)
    rank_wanted = lax.rem(column, PM).astype(F32)
    below = (
        lax.broadcasted_iota(jnp.int32, (TT, TT), 1) < lax.broadcasted_iota(jnp.int32, (TT, TT), 0)
    ).astype(F32).astype(BF)
    group_lane = lax.broadcasted_iota(jnp.int32, (TT, 128), 1) - OFF
    row_lane = lax.broadcasted_iota(jnp.int32, (LR, 128), 1) - OFF

    for jg in range(NG):
        group = groups[jg]
        for j in range(max(1, jg * G), (jg + 1) * G):
            await_strided(0, gathered, z_send, z_recv, j)
            send_strided(1, j)
        block = gathered[0, pl.ds(group * G, G)].reshape(TT, DP)
        route = block[:, TB:].astype(F32)

        def lane_of(i, k):
            return route[:, OFF + i * TOP + k : OFF + i * TOP + k + 1]

        hits = []
        for k in range(TOP):
            hit = (lane_of(0, k) == wanted) & (lane_of(1, k) > 0.0) & same_source
            hits.append(hit.astype(F32))
        hit_any = sum(hits)
        rank = contract(below, hit_any.astype(BF), 1, 0)
        picked = jnp.where(rank == rank_wanted, hit_any, 0.0)
        picked_bf = picked.astype(BF)
        select[group] = picked_bf
        moved = contract(picked_bf, block, 0, 0)
        info = jnp.zeros((LR, 128), F32)
        for k in range(TOP):
            values = jnp.where(group_lane == 0, lane_of(1, k), 0.0)
            values = jnp.where(group_lane == 1, float(k), values)
            for i in range(3):
                values = jnp.where(group_lane == 2 + i, lane_of(2 + i, k), values)
            info = info + contract((picked * hits[k]).astype(BF), values.astype(BF), 0, 0)
        plane_out[0, group, :, :, :TB] = moved[:, :TB].astype(BF).reshape(L, R, TB)
        plane_out[0, group, :, :, TB:] = (
            jnp.where(row_lane < 0, moved[:, TB:], info).astype(BF).reshape(L, R, 128)
        )
        send_local(0, plane_out, plane_in, p_send, p_recv, group)

    for jg in range(NG):
        group = groups[jg]
        for j in range(max(1, jg * G), (jg + 1) * G):
            await_strided(1, gathered, z_send, z_recv, j)
        block = gathered[1, pl.ds(group * G, G)].reshape(TT, DP)
        moved = contract(select[group], block, 0, 0)
        plane_out[1, group] = moved.astype(BF).reshape(L, R, DP)
        send_local(1, plane_out, plane_in, p_send, p_recv, group)

    def swap(index, source, target):
        copy = send(source, target, c_send.at[index], c_recv.at[index], (l, s, twin))
        return copy

    middle = -(-D // 256) * 128
    halves = ((0, middle), (middle, D))

    def swap_half(kind, c):
        low, high = halves[c]
        index = 2 + 2 * kind + c
        swap(
            index,
            partial.at[kind, twin, :, pl.ds(low, high - low)],
            other.at[kind, :, pl.ds(low, high - low)],
        )

    def await_half(kind, c):
        low, high = halves[c]
        index = 2 + 2 * kind + c
        arrival(
            other.at[kind, :, pl.ds(low, high - low)],
            c_send.at[index],
            c_recv.at[index],
            (l, s, twin),
        ).wait_recv()

    saves = []

    def save(index, source, target):
        copy = pltpu.make_async_copy(source, target, d_sem.at[index])
        copy.start()
        saves.append(copy)

    def await_plane(kind):
        for jg in range(NG):
            for j in range(1, L):
                await_local(kind, plane_in, p_send, p_recv, groups[jg], j)

    await_plane(0)
    received = plane_in[0].reshape(NG * LR, DP)
    slot_of = received[:, TB:].astype(F32)[:, OFF : OFF + 1]
    slot_lane = lax.broadcasted_iota(jnp.int32, (NG * LR, CAP), 1).astype(F32) + 1.0
    place[...] = (slot_of == slot_lane).astype(F32).astype(BF)
    rows[0, r] = contract(place[...], received, 0, 0).astype(BF)
    swap(0, rows.at[0, r], rows.at[0, r])
    for load in loads:
        load.wait()
    arrival(rows.at[0, twin], c_send.at[0], c_recv.at[0], (l, s, twin)).wait_recv()

    x = rows[0].reshape(2 * CAP, DP)[:, :D]
    gate = contract(x, w_gate[...], 1, 0)
    gate_pre[...] = gate
    up = contract(x, w_up[...], 1, 0)
    up_pre[...] = up
    hidden[...] = ((up + 1.0) * gate * jax.nn.sigmoid(SWIGLU_ALPHA * gate)).astype(BF)
    save(2, hidden, hidden_hbm)
    save(0, rows.at[0], rows_hbm)
    for c, (low, high) in enumerate(halves):
        part = contract(hidden[...], w_down[:, low:high], 1, 0)
        partial[0, :, :, low:high] = part.reshape(2, CAP, high - low)
        swap_half(0, c)

    def weight_of(tail):
        return (
            tail[:, OFF + 2 : OFF + 3] + tail[:, OFF + 3 : OFF + 4] + tail[:, OFF + 4 : OFF + 5]
        )

    weight_rows = weight_of(rows[0].reshape(2 * CAP, DP)[:, TB:].astype(F32))
    own_tail = rows[0, r, :, TB:].astype(F32)
    await_half(0, 0)
    await_half(0, 1)
    out = partial[0, r] + other[0]
    reply[0, :, TB:] = jnp.zeros((CAP, 128), BF)
    reply[0, :, :D] = (weight_of(own_tail) * out).astype(BF)
    back_out[0] = contract(place[...], reply[0], 1, 0).astype(BF).reshape(NG, L, R, DP)
    for jg in reversed(range(NG)):
        send_local(0, back_out, back_in, r_send, r_recv, groups[jg])

    await_plane(1)
    rows[1, r] = contract(place[...], plane_in[1].reshape(NG * LR, DP), 0, 0).astype(BF)
    swap(1, rows.at[1, r], rows.at[1, r])
    own_grads = rows[1, r, :, :D].astype(F32)
    router_grad = jnp.sum(own_grads * out, axis=1, keepdims=True)
    slot_tail = lax.broadcasted_iota(jnp.int32, (CAP, 128), 1).astype(F32) - float(OFF)
    which = own_tail[:, OFF + 1 : OFF + 2]
    reply_tail = jnp.zeros((CAP, 128), F32)
    for i, part in enumerate(three_parts(router_grad)):
        reply_tail = jnp.where(slot_tail == which + float(i * TOP), part, reply_tail)
    arrival(rows.at[1, twin], c_send.at[1], c_recv.at[1], (l, s, twin)).wait_recv()
    grads[...] = (weight_rows * rows[1].reshape(2 * CAP, DP)[:, :D].astype(F32)).astype(BF)
    grad_hidden = contract(grads[...], w_down[...], 1, 1)
    gate = gate_pre[...]
    sig = jax.nn.sigmoid(SWIGLU_ALPHA * gate)
    slope_up[...] = (grad_hidden * gate * sig).astype(BF)
    slope = sig + SWIGLU_ALPHA * gate * sig * (1.0 - sig)
    slope_gate[...] = (grad_hidden * (up_pre[...] + 1.0) * slope).astype(BF)
    for c, (low, high) in enumerate(halves):
        part = contract(slope_gate[...], w_gate[low:high, :], 1, 1) + contract(
            slope_up[...], w_up[low:high, :], 1, 1
        )
        partial[1, :, :, low:high] = part.reshape(2, CAP, high - low)
        swap_half(1, c)
    save(1, grads, grads_hbm)
    save(3, slope_gate, slope_gate_hbm)
    save(4, slope_up, slope_up_hbm)
    await_half(1, 0)
    await_half(1, 1)
    reply[1, :, TB:] = jnp.zeros((CAP, 128), BF)
    reply[1, :, :D] = (partial[1, r] + other[1]).astype(BF)
    reply[1, :, TB:] = jnp.where(
        slot_tail < 0.0, reply[1, :, TB:].astype(F32), reply_tail
    ).astype(BF)
    back_out[1] = contract(place[...], reply[1], 1, 0).astype(BF).reshape(NG, L, R, DP)
    for jg in reversed(range(NG)):
        send_local(1, back_out, back_in, r_send, r_recv, groups[jg])

    def send_home(kind):
        for jg in reversed(range(NG)):
            group = groups[jg]
            for j in range(1, L):
                await_local(kind, back_in, r_send, r_recv, group, j)
            total = contract(select[group], back_in[kind, group].reshape(LR, DP), 1, 0)
            home_out[kind, pl.ds(group * G, G)] = total.astype(BF).reshape(G, T, DP)
            for j in range(jg * G, (jg + 1) * G):
                peer = strided_peers[j]
                if j == 0:
                    home_in[kind, s] = home_out[kind, s]
                else:
                    send(
                        home_out.at[kind, peer],
                        home_in.at[kind, s],
                        h_send.at[kind, j],
                        h_recv.at[kind, s],
                        (l, peer, r),
                    )

    send_home(0)
    send_home(1)

    def collect(kind):
        for j in range(1, S):
            await_strided(kind, home_in, h_send, h_recv, j)
        total = home_in[kind, 0].astype(F32)
        for j in range(1, S):
            total = total + home_in[kind, j].astype(F32)
        return total

    mixed[0] = collect(0)[:, :D].astype(BF)
    total = collect(1)
    token_grad[0] = total[:, :D].astype(BF)
    line = lax.broadcasted_iota(jnp.int32, (16, 128), 0)
    spot = lax.broadcasted_iota(jnp.int32, (16, 128), 1) - OFF
    chosen = (spot >= 0) & (spot < 3 * TOP) & (lax.rem(spot + 128, TOP) == line)
    weight_grad[0] = contract(
        chosen.astype(F32).astype(BF), total[:, TB:].astype(BF), 1, 1
    )[:TOP]
    for copy in saves:
        copy.wait()
    for copy in pending:
        copy.wait_send()


def weight_kernel(
    sizes,
    rows_hbm,
    grads_hbm,
    hidden_hbm,
    slope_gate_hbm,
    slope_up_hbm,
    mixed_in,
    token_grad_in,
    weight_grad_in,
    mixed,
    token_grad,
    weight_grad,
    gate_grad_hbm,
    up_grad_hbm,
    down_grad_hbm,
    rows,
    grads,
    hidden,
    slope_gate,
    slope_up,
    d_gate,
    d_up,
    d_down,
    in_sem,
    out_sem,
):
    D, DP, CAP, step = sizes
    F = hidden.shape[1]
    pairs = (
        (rows_hbm, rows),
        (slope_gate_hbm, slope_gate),
        (slope_up_hbm, slope_up),
        (grads_hbm, grads),
        (hidden_hbm, hidden),
    )
    loads = [
        pltpu.make_async_copy(source, target, in_sem.at[i])
        for i, (source, target) in enumerate(pairs)
    ]
    for load in loads:
        load.start()
    mixed[...] = mixed_in[...]
    token_grad[...] = token_grad_in[...]
    weight_grad[...] = weight_grad_in[...]
    stores = []

    def fill(left, right, target, out, limit):
        for low in range(0, limit, step):
            size = min(step, limit - low)
            target[low : low + size, :] = contract(
                left(low, low + size), right[...], 0, 0
            ).astype(BF)
            copy = pltpu.make_async_copy(
                target.at[pl.ds(low, size)],
                out.at[0, pl.ds(low, size)],
                out_sem.at[len(stores)],
            )
            copy.start()
            stores.append(copy)

    def row_columns(low, high):
        return rows[:, :, low:high].reshape(2 * CAP, high - low)

    loads[0].wait()
    loads[1].wait()
    fill(row_columns, slope_gate, d_gate, gate_grad_hbm, D)
    loads[2].wait()
    fill(row_columns, slope_up, d_up, up_grad_hbm, D)
    loads[3].wait()
    loads[4].wait()
    fill(lambda low, high: hidden[:, low:high], grads, d_down, down_grad_hbm, F)
    for copy in stores:
        copy.wait()


def local(tokens, experts, slots, route_weight, out_grad, w_gate, w_up, w_down):
    L, S = lax.axis_size("local"), lax.axis_size("strided")
    T, D = tokens.shape[1:]
    TOP = experts.shape[2]
    F = w_gate.shape[2]
    CAP = T * TOP
    PM = 2 * CAP // (L * S)
    G = max(1, 16 // PM)
    R = G * PM
    NG, TT, LR = S // G, G * T, L * R
    DP = -(-(D + 5 * TOP) // 128) * 128
    sizes = (S, L, T, TOP, PM, G, R, D, DP, CAP)
    vmem = pl.BlockSpec(memory_space=pltpu.VMEM)
    anywhere = pl.BlockSpec(memory_space=pl.ANY)
    dma = pltpu.SemaphoreType.DMA
    by_choice = [jnp.swapaxes(a, 1, 2) for a in (experts, slots, route_weight)]
    returned = (
        jax.ShapeDtypeStruct((1, T, D), BF),
        jax.ShapeDtypeStruct((1, T, D), BF),
        jax.ShapeDtypeStruct((1, TOP, T), F32),
    )
    kept = (
        jax.ShapeDtypeStruct((2, CAP, DP), BF),
        jax.ShapeDtypeStruct((2 * CAP, D), BF),
        jax.ShapeDtypeStruct((2 * CAP, F), BF),
        jax.ShapeDtypeStruct((2 * CAP, F), BF),
        jax.ShapeDtypeStruct((2 * CAP, F), BF),
    )
    results = pl.pallas_call(
        functools.partial(kernel, sizes),
        out_shape=returned + kept,
        in_specs=[vmem] * 5 + [anywhere] * 3,
        out_specs=[vmem] * 3 + [anywhere] * 5,
        scratch_shapes=[
            pltpu.VMEM((D, F), BF),
            pltpu.VMEM((D, F), BF),
            pltpu.VMEM((F, D), BF),
            pltpu.VMEM((80, T), F32),
            pltpu.VMEM((2, S, T, DP), BF),
            pltpu.VMEM((2, NG, L, R, DP), BF),
            pltpu.VMEM((2, NG, L, R, DP), BF),
            pltpu.VMEM((2, NG, L, R, DP), BF),
            pltpu.VMEM((2, NG, L, R, DP), BF),
            pltpu.VMEM((2, S, T, DP), BF),
            pltpu.VMEM((2, S, T, DP), BF),
            pltpu.VMEM((NG, TT, LR), BF),
            pltpu.VMEM((NG * LR, CAP), BF),
            pltpu.VMEM((2, 2, CAP, DP), BF),
            pltpu.VMEM((2 * CAP, D), BF),
            pltpu.VMEM((2 * CAP, F), BF),
            pltpu.VMEM((2 * CAP, F), F32),
            pltpu.VMEM((2 * CAP, F), F32),
            pltpu.VMEM((2 * CAP, F), BF),
            pltpu.VMEM((2 * CAP, F), BF),
            pltpu.VMEM((2, 2, CAP, D), F32),
            pltpu.VMEM((2, CAP, D), F32),
            pltpu.VMEM((2, CAP, DP), BF),
            dma((3,)),
            dma((5,)),
            dma((2, S)),
            dma((2, S)),
            dma((2, NG, L)),
            dma((2, NG, L)),
            dma((2, NG, L)),
            dma((2, NG, L)),
            dma((2, S)),
            dma((2, S)),
            dma((6,)),
            dma((6,)),
        ],
        compiler_params=pltpu.CompilerParams(
            collective_id=0, has_side_effects=True, vmem_limit_bytes=58 * 1024 * 1024
        ),
        cost_estimate=pl.CostEstimate(
            flops=12 * 2 * CAP * D * F, bytes_accessed=6 * D * F, transcendentals=4 * CAP * F
        ),
        name="moe_layer",
    )(tokens, *by_choice, out_grad, w_gate, w_up, w_down)
    step = 512
    copies = 2 * -(-D // step) + -(-F // step)
    mixed, token_grad, weight_grad, gate_grad, up_grad, down_grad = pl.pallas_call(
        functools.partial(weight_kernel, (D, DP, CAP, step)),
        out_shape=returned
        + (
            jax.ShapeDtypeStruct((1, D, F), BF),
            jax.ShapeDtypeStruct((1, D, F), BF),
            jax.ShapeDtypeStruct((1, F, D), BF),
        ),
        in_specs=[anywhere] * 5 + [vmem] * 3,
        out_specs=[vmem] * 3 + [anywhere] * 3,
        scratch_shapes=[pltpu.VMEM(a.shape, a.dtype) for a in kept]
        + [
            pltpu.VMEM((D, F), BF),
            pltpu.VMEM((D, F), BF),
            pltpu.VMEM((F, D), BF),
            dma((5,)),
            dma((copies,)),
        ],
        compiler_params=pltpu.CompilerParams(vmem_limit_bytes=60 * 1024 * 1024),
        cost_estimate=pl.CostEstimate(
            flops=6 * 2 * CAP * D * F, bytes_accessed=6 * D * F, transcendentals=0
        ),
        name="weight_grads",
    )(*results[3:], *results[:3])
    return mixed, token_grad, jnp.swapaxes(weight_grad, 1, 2), gate_grad, up_grad, down_grad


def solution(mesh):
    pairs = P("rep", ("local", "strided"), None)
    split_last = P(("local", "strided"), None, "rep")
    split_middle = P(("local", "strided"), "rep", None)
    return jax.shard_map(
        local,
        mesh=mesh,
        in_specs=(pairs,) * 5 + (split_last, split_last, split_middle),
        out_specs=(pairs,) * 3 + (split_last, split_last, split_middle),
        check_vma=False,
    )
```

```python
import functools

import jax
import jax.numpy as jnp
from jax import lax
from jax.experimental import pallas as pl
from jax.experimental.pallas import tpu as pltpu
from jax.sharding import PartitionSpec as P

SWIGLU_ALPHA = 1.702
BF = jnp.bfloat16
F32 = jnp.float32
MESH = pl.DeviceIdType.MESH


def contract(left, right, left_dim, right_dim):
    return lax.dot_general(
        left, right, (((left_dim,), (right_dim,)), ((), ())), preferred_element_type=F32
    )


def xor(index, constant, size):
    result, bit = 0, 1
    while bit < size:
        result = result + bit * lax.rem(lax.div(index, bit) + (constant // bit) % 2, 2)
        bit *= 2
    return result


def three_parts(value):
    high = value.astype(BF).astype(F32)
    middle = (value - high).astype(BF).astype(F32)
    low = (value - high - middle).astype(BF).astype(F32)
    return high, middle, low


def kernel(
    sizes,
    tokens,
    experts,
    slots,
    router,
    out_grad,
    gate_hbm,
    up_hbm,
    down_hbm,
    mixed,
    token_grad,
    weight_grad,
    rows_hbm,
    grads_hbm,
    hidden_hbm,
    slope_gate_hbm,
    slope_up_hbm,
    w_gate,
    w_up,
    w_down,
    rows_t,
    hidden_t,
    routing,
    gathered,
    plane_out,
    plane_in,
    back_out,
    back_in,
    home_out,
    home_in,
    select,
    place,
    rows,
    grads,
    hidden,
    gate_pre,
    up_pre,
    slope_gate,
    slope_up,
    partial,
    other,
    reply,
    w_sem,
    d_sem,
    z_send,
    z_recv,
    p_send,
    p_recv,
    r_send,
    r_recv,
    h_send,
    h_recv,
    c_send,
    c_recv,
):
    S, L, T, TOP, PM, G, R, D, DP, CAP = sizes
    NG, TT, LR = S // G, G * T, L * R
    TB = DP - 128
    OFF = D - TB
    l, s, r = lax.axis_index("local"), lax.axis_index("strided"), lax.axis_index("rep")
    twin = 1 - r
    strided_peers = [xor(s, j, S) for j in range(S)]
    local_peers = [xor(l, j, L) for j in range(L)]
    groups = [xor(lax.div(s, G), j, NG) for j in range(NG)]

    loads = [
        pltpu.make_async_copy(source.at[0], target, w_sem.at[i])
        for i, (source, target) in enumerate(
            ((gate_hbm, w_gate), (up_hbm, w_up), (down_hbm, w_down))
        )
    ]
    for load in loads:
        load.start()

    barrier = pltpu.get_barrier_semaphore()
    for j in range(1, S):
        pl.semaphore_signal(
            barrier, inc=1, device_id=(l, strided_peers[j], r), device_id_type=MESH
        )
    for j in range(1, L):
        pl.semaphore_signal(barrier, inc=1, device_id=(local_peers[j], s, r), device_id_type=MESH)
    pl.semaphore_signal(barrier, inc=1, device_id=(l, s, twin), device_id_type=MESH)

    lane = lax.broadcasted_iota(jnp.int32, (T, 128), 1) - OFF
    gathered[0, s, :, TB:] = jnp.zeros((T, 128), BF)
    gathered[1, s, :, TB:] = jnp.zeros((T, 128), BF)
    gathered[0, s, :, :D] = tokens[0]
    gathered[1, s, :, :D] = out_grad[0]
    routing[...] = jnp.zeros(routing.shape, F32)
    parts = (experts[0].astype(F32), slots[0].astype(F32) + 1.0) + three_parts(router[0])
    for i, part in enumerate(parts):
        routing[i * 16 : i * 16 + TOP, :] = part
    line = lax.broadcasted_iota(jnp.int32, (80, 128), 0)
    spot = lax.broadcasted_iota(jnp.int32, (80, 128), 1) - OFF
    spread = (lax.rem(line, 16) < TOP) & (spot == lax.div(line, 16) * TOP + lax.rem(line, 16))
    info = contract(routing[...].astype(BF), spread.astype(F32).astype(BF), 0, 0)
    tail = gathered[0, s, :, TB:].astype(F32)
    gathered[0, s, :, TB:] = jnp.where(lane < 0, tail, info).astype(BF)

    pl.semaphore_wait(barrier, (S - 1) + (L - 1) + 1)

    pending = []

    def send(source, target, send_sem, recv_sem, device):
        copy = pltpu.make_async_remote_copy(
            src_ref=source,
            dst_ref=target,
            send_sem=send_sem,
            recv_sem=recv_sem,
            device_id=device,
            device_id_type=MESH,
        )
        copy.start()
        pending.append(copy)
        return copy

    def arrival(target, send_sem, recv_sem, device):
        return pltpu.make_async_remote_copy(
            src_ref=target,
            dst_ref=target,
            send_sem=send_sem,
            recv_sem=recv_sem,
            device_id=device,
            device_id_type=MESH,
        )

    def send_strided(kind, j):
        send(
            gathered.at[kind, s],
            gathered.at[kind, s],
            z_send.at[kind, j],
            z_recv.at[kind, s],
            (l, strided_peers[j], r),
        )

    for j in range(1, S):
        send_strided(0, j)

    def await_strided(kind, buffer, sends, recvs, j):
        peer = strided_peers[j]
        arrival(
            buffer.at[kind, peer], sends.at[kind, j], recvs.at[kind, peer], (l, peer, r)
        ).wait_recv()

    def await_local(kind, buffer, sends, recvs, group, j):
        peer = local_peers[j]
        arrival(
            buffer.at[kind, group, peer],
            sends.at[kind, group, j],
            recvs.at[kind, group, peer],
            (peer, s, r),
        ).wait_recv()

    def send_local(kind, outgoing, incoming, sends, recvs, group):
        for j in range(1, L):
            send(
                outgoing.at[kind, group, local_peers[j]],
                incoming.at[kind, group, l],
                sends.at[kind, group, j],
                recvs.at[kind, group, l],
                (local_peers[j], s, r),
            )
        incoming[kind, group, l] = outgoing[kind, group, l]

    column = lax.broadcasted_iota(jnp.int32, (TT, LR), 1)
    token = lax.broadcasted_iota(jnp.int32, (TT, LR), 0)
    wanted = (lax.div(column, R) * S + s).astype(F32)
    same_source = lax.div(token, T) == lax.div(lax.rem(column, R), PM)
    rank_wanted = lax.rem(column, PM).astype(F32)
    below = (
        lax.broadcasted_iota(jnp.int32, (TT, TT), 1) < lax.broadcasted_iota(jnp.int32, (TT, TT), 0)
    ).astype(F32).astype(BF)
    group_lane = lax.broadcasted_iota(jnp.int32, (TT, 128), 1) - OFF
    row_lane = lax.broadcasted_iota(jnp.int32, (LR, 128), 1) - OFF

    for jg in range(NG):
        group = groups[jg]
        for j in range(max(1, jg * G), (jg + 1) * G):
            await_strided(0, gathered, z_send, z_recv, j)
            send_strided(1, j)
        block = gathered[0, pl.ds(group * G, G)].reshape(TT, DP)
        route = block[:, TB:].astype(F32)

        def lane_of(i, k):
            return route[:, OFF + i * TOP + k : OFF + i * TOP + k + 1]

        hits = []
        for k in range(TOP):
            hit = (lane_of(0, k) == wanted) & (lane_of(1, k) > 0.0) & same_source
            hits.append(hit.astype(F32))
        hit_any = sum(hits)
        rank = contract(below, hit_any.astype(BF), 1, 0)
        picked = jnp.where(rank == rank_wanted, hit_any, 0.0)
        picked_bf = picked.astype(BF)
        select[group] = picked_bf
        moved = contract(picked_bf, block, 0, 0)
        info = jnp.zeros((LR, 128), F32)
        for k in range(TOP):
            values = jnp.where(group_lane == 0, lane_of(1, k), 0.0)
            values = jnp.where(group_lane == 1, float(k), values)
            for i in range(3):
                values = jnp.where(group_lane == 2 + i, lane_of(2 + i, k), values)
            info = info + contract((picked * hits[k]).astype(BF), values.astype(BF), 0, 0)
        plane_out[0, group, :, :, :TB] = moved[:, :TB].astype(BF).reshape(L, R, TB)
        plane_out[0, group, :, :, TB:] = (
            jnp.where(row_lane < 0, moved[:, TB:], info).astype(BF).reshape(L, R, 128)
        )
        send_local(0, plane_out, plane_in, p_send, p_recv, group)

    for jg in range(NG):
        group = groups[jg]
        for j in range(max(1, jg * G), (jg + 1) * G):
            await_strided(1, gathered, z_send, z_recv, j)
        block = gathered[1, pl.ds(group * G, G)].reshape(TT, DP)
        moved = contract(select[group], block, 0, 0)
        plane_out[1, group] = moved.astype(BF).reshape(L, R, DP)
        send_local(1, plane_out, plane_in, p_send, p_recv, group)

    def swap(index, source, target):
        copy = send(source, target, c_send.at[index], c_recv.at[index], (l, s, twin))
        return copy

    middle = -(-D // 256) * 128
    halves = ((0, middle), (middle, D))

    def swap_half(kind, c):
        low, high = halves[c]
        index = 2 + 2 * kind + c
        swap(
            index,
            partial.at[kind, twin, :, pl.ds(low, high - low)],
            other.at[kind, :, pl.ds(low, high - low)],
        )

    def await_half(kind, c):
        low, high = halves[c]
        index = 2 + 2 * kind + c
        arrival(
            other.at[kind, :, pl.ds(low, high - low)],
            c_send.at[index],
            c_recv.at[index],
            (l, s, twin),
        ).wait_recv()

    saves = []

    def save(index, source, target):
        copy = pltpu.make_async_copy(source, target, d_sem.at[index])
        copy.start()
        saves.append(copy)

    slot_lane = lax.broadcasted_iota(jnp.int32, (LR, CAP), 1).astype(F32) + 1.0

    def compact(kind):
        total = jnp.zeros((CAP, DP), F32)
        for jg in range(NG):
            group = groups[jg]
            for j in range(1, L):
                await_local(kind, plane_in, p_send, p_recv, group, j)
            received = plane_in[kind, group].reshape(LR, DP)
            if kind == 0:
                slot_of = received[:, TB:].astype(F32)[:, OFF : OFF + 1]
                place[group] = (slot_of == slot_lane).astype(F32).astype(BF)
            total = total + contract(place[group], received, 0, 0)
        rows[kind, r] = total.astype(BF)

    def send_back(kind):
        for jg in reversed(range(NG)):
            group = groups[jg]
            spread_rows = contract(place[group], reply[kind], 1, 0)
            back_out[kind, group] = spread_rows.astype(BF).reshape(L, R, DP)
            send_local(kind, back_out, back_in, r_send, r_recv, group)

    compact(0)
    swap(0, rows.at[0, r], rows.at[0, r])
    for load in loads:
        load.wait()
    arrival(rows.at[0, twin], c_send.at[0], c_recv.at[0], (l, s, twin)).wait_recv()

    x = rows[0].reshape(2 * CAP, DP)[:, :D]
    gate = contract(x, w_gate[...], 1, 0)
    gate_pre[...] = gate
    up = contract(x, w_up[...], 1, 0)
    up_pre[...] = up
    hidden[...] = ((up + 1.0) * gate * jax.nn.sigmoid(SWIGLU_ALPHA * gate)).astype(BF)
    for c, (low, high) in enumerate(halves):
        part = contract(hidden[...], w_down[:, low:high], 1, 0)
        partial[0, :, :, low:high] = part.reshape(2, CAP, high - low)
        swap_half(0, c)

    def weight_of(tail):
        return (
            tail[:, OFF + 2 : OFF + 3] + tail[:, OFF + 3 : OFF + 4] + tail[:, OFF + 4 : OFF + 5]
        )

    weight_rows = weight_of(rows[0].reshape(2 * CAP, DP)[:, TB:].astype(F32))
    own_tail = rows[0, r, :, TB:].astype(F32)
    await_half(0, 0)
    await_half(0, 1)
    out = partial[0, r] + other[0]
    reply[0, :, TB:] = jnp.zeros((CAP, 128), BF)
    reply[0, :, :D] = (weight_of(own_tail) * out).astype(BF)
    send_back(0)

    compact(1)
    swap(1, rows.at[1, r], rows.at[1, r])
    own_grads = rows[1, r, :, :D].astype(F32)
    router_grad = jnp.sum(own_grads * out, axis=1, keepdims=True)
    slot_tail = lax.broadcasted_iota(jnp.int32, (CAP, 128), 1).astype(F32) - float(OFF)
    which = own_tail[:, OFF + 1 : OFF + 2]
    reply_tail = jnp.zeros((CAP, 128), F32)
    for i, part in enumerate(three_parts(router_grad)):
        reply_tail = jnp.where(slot_tail == which + float(i * TOP), part, reply_tail)
    arrival(rows.at[1, twin], c_send.at[1], c_recv.at[1], (l, s, twin)).wait_recv()
    grads[...] = (weight_rows * rows[1].reshape(2 * CAP, DP)[:, :D].astype(F32)).astype(BF)
    grad_hidden = contract(grads[...], w_down[...], 1, 1)
    gate = gate_pre[...]
    sig = jax.nn.sigmoid(SWIGLU_ALPHA * gate)
    slope_up[...] = (grad_hidden * gate * sig).astype(BF)
    slope = sig + SWIGLU_ALPHA * gate * sig * (1.0 - sig)
    slope_gate[...] = (grad_hidden * (up_pre[...] + 1.0) * slope).astype(BF)
    for c, (low, high) in enumerate(halves):
        part = contract(slope_gate[...], w_gate[low:high, :], 1, 1) + contract(
            slope_up[...], w_up[low:high, :], 1, 1
        )
        partial[1, :, :, low:high] = part.reshape(2, CAP, high - low)
        swap_half(1, c)
    save(1, grads, grads_hbm)
    save(3, slope_gate, slope_gate_hbm)
    save(4, slope_up, slope_up_hbm)
    await_half(1, 0)
    await_half(1, 1)
    reply[1, :, TB:] = jnp.zeros((CAP, 128), BF)
    reply[1, :, :D] = (partial[1, r] + other[1]).astype(BF)
    reply[1, :, TB:] = jnp.where(
        slot_tail < 0.0, reply[1, :, TB:].astype(F32), reply_tail
    ).astype(BF)
    send_back(1)

    def send_home(kind):
        for jg in reversed(range(NG)):
            group = groups[jg]
            for j in range(1, L):
                await_local(kind, back_in, r_send, r_recv, group, j)
            total = contract(select[group], back_in[kind, group].reshape(LR, DP), 1, 0)
            home_out[kind, pl.ds(group * G, G)] = total.astype(BF).reshape(G, T, DP)
            for j in range(jg * G, (jg + 1) * G):
                peer = strided_peers[j]
                if j == 0:
                    home_in[kind, s] = home_out[kind, s]
                else:
                    send(
                        home_out.at[kind, peer],
                        home_in.at[kind, s],
                        h_send.at[kind, j],
                        h_recv.at[kind, s],
                        (l, peer, r),
                    )

    rows_t[...] = rows[0].reshape(2 * CAP, DP).T
    save(0, rows_t, rows_hbm)
    hidden_t[...] = hidden[...].T
    save(2, hidden_t, hidden_hbm)
    send_home(0)
    send_home(1)

    def collect(kind):
        for j in range(1, S):
            await_strided(kind, home_in, h_send, h_recv, j)
        total = home_in[kind, 0].astype(F32)
        for j in range(1, S):
            total = total + home_in[kind, j].astype(F32)
        return total

    mixed[0] = collect(0)[:, :D].astype(BF)
    total = collect(1)
    token_grad[0] = total[:, :D].astype(BF)
    line = lax.broadcasted_iota(jnp.int32, (16, 128), 0)
    spot = lax.broadcasted_iota(jnp.int32, (16, 128), 1) - OFF
    chosen = (spot >= 0) & (spot < 3 * TOP) & (lax.rem(spot + 128, TOP) == line)
    weight_grad[0] = contract(
        chosen.astype(F32).astype(BF), total[:, TB:].astype(BF), 1, 1
    )[:TOP]
    for copy in saves:
        copy.wait()
    for copy in pending:
        copy.wait_send()


def weight_kernel(
    sizes,
    rows_hbm,
    grads_hbm,
    hidden_hbm,
    slope_gate_hbm,
    slope_up_hbm,
    mixed_in,
    token_grad_in,
    weight_grad_in,
    mixed,
    token_grad,
    weight_grad,
    gate_grad_hbm,
    up_grad_hbm,
    down_grad_hbm,
    rows,
    grads,
    hidden,
    slope_gate,
    slope_up,
    d_gate,
    d_up,
    d_down,
    in_sem,
    out_sem,
):
    D, DP, CAP, step = sizes
    F = hidden.shape[0]
    pairs = (
        (rows_hbm, rows),
        (slope_gate_hbm, slope_gate),
        (slope_up_hbm, slope_up),
        (grads_hbm, grads),
        (hidden_hbm, hidden),
    )
    loads = [
        pltpu.make_async_copy(source, target, in_sem.at[i])
        for i, (source, target) in enumerate(pairs)
    ]
    for load in loads:
        load.start()
    mixed[...] = mixed_in[...]
    token_grad[...] = token_grad_in[...]
    weight_grad[...] = weight_grad_in[...]
    stores = []

    def fill(left, right, target, out, limit):
        for low in range(0, limit, step):
            size = min(step, limit - low)
            target[low : low + size, :] = contract(
                left[low : low + size, :], right[...], 1, 0
            ).astype(BF)
            copy = pltpu.make_async_copy(
                target.at[pl.ds(low, size)],
                out.at[0, pl.ds(low, size)],
                out_sem.at[len(stores)],
            )
            copy.start()
            stores.append(copy)

    loads[0].wait()
    loads[1].wait()
    fill(rows, slope_gate, d_gate, gate_grad_hbm, D)
    loads[2].wait()
    fill(rows, slope_up, d_up, up_grad_hbm, D)
    loads[3].wait()
    loads[4].wait()
    fill(hidden, grads, d_down, down_grad_hbm, F)
    for copy in stores:
        copy.wait()


def local(tokens, experts, slots, route_weight, out_grad, w_gate, w_up, w_down):
    L, S = lax.axis_size("local"), lax.axis_size("strided")
    T, D = tokens.shape[1:]
    TOP = experts.shape[2]
    F = w_gate.shape[2]
    CAP = T * TOP
    PM = 2 * CAP // (L * S)
    G = max(1, 16 // PM)
    R = G * PM
    NG, TT, LR = S // G, G * T, L * R
    DP = -(-(D + 5 * TOP) // 128) * 128
    sizes = (S, L, T, TOP, PM, G, R, D, DP, CAP)
    vmem = pl.BlockSpec(memory_space=pltpu.VMEM)
    anywhere = pl.BlockSpec(memory_space=pl.ANY)
    dma = pltpu.SemaphoreType.DMA
    by_choice = [jnp.swapaxes(a, 1, 2) for a in (experts, slots, route_weight)]
    returned = (
        jax.ShapeDtypeStruct((1, T, D), BF),
        jax.ShapeDtypeStruct((1, T, D), BF),
        jax.ShapeDtypeStruct((1, TOP, T), F32),
    )
    kept = (
        jax.ShapeDtypeStruct((DP, 2 * CAP), BF),
        jax.ShapeDtypeStruct((2 * CAP, D), BF),
        jax.ShapeDtypeStruct((F, 2 * CAP), BF),
        jax.ShapeDtypeStruct((2 * CAP, F), BF),
        jax.ShapeDtypeStruct((2 * CAP, F), BF),
    )
    results = pl.pallas_call(
        functools.partial(kernel, sizes),
        out_shape=returned + kept,
        in_specs=[vmem] * 5 + [anywhere] * 3,
        out_specs=[vmem] * 3 + [anywhere] * 5,
        scratch_shapes=[
            pltpu.VMEM((D, F), BF),
            pltpu.VMEM((D, F), BF),
            pltpu.VMEM((F, D), BF),
            pltpu.VMEM((DP, 2 * CAP), BF),
            pltpu.VMEM((F, 2 * CAP), BF),
            pltpu.VMEM((80, T), F32),
            pltpu.VMEM((2, S, T, DP), BF),
            pltpu.VMEM((2, NG, L, R, DP), BF),
            pltpu.VMEM((2, NG, L, R, DP), BF),
            pltpu.VMEM((2, NG, L, R, DP), BF),
            pltpu.VMEM((2, NG, L, R, DP), BF),
            pltpu.VMEM((2, S, T, DP), BF),
            pltpu.VMEM((2, S, T, DP), BF),
            pltpu.VMEM((NG, TT, LR), BF),
            pltpu.VMEM((NG, LR, CAP), BF),
            pltpu.VMEM((2, 2, CAP, DP), BF),
            pltpu.VMEM((2 * CAP, D), BF),
            pltpu.VMEM((2 * CAP, F), BF),
            pltpu.VMEM((2 * CAP, F), F32),
            pltpu.VMEM((2 * CAP, F), F32),
            pltpu.VMEM((2 * CAP, F), BF),
            pltpu.VMEM((2 * CAP, F), BF),
            pltpu.VMEM((2, 2, CAP, D), F32),
            pltpu.VMEM((2, CAP, D), F32),
            pltpu.VMEM((2, CAP, DP), BF),
            dma((3,)),
            dma((5,)),
            dma((2, S)),
            dma((2, S)),
            dma((2, NG, L)),
            dma((2, NG, L)),
            dma((2, NG, L)),
            dma((2, NG, L)),
            dma((2, S)),
            dma((2, S)),
            dma((6,)),
            dma((6,)),
        ],
        compiler_params=pltpu.CompilerParams(
            collective_id=0, has_side_effects=True, vmem_limit_bytes=58 * 1024 * 1024
        ),
        cost_estimate=pl.CostEstimate(
            flops=12 * 2 * CAP * D * F, bytes_accessed=6 * D * F, transcendentals=4 * CAP * F
        ),
        name="moe_layer",
    )(tokens, *by_choice, out_grad, w_gate, w_up, w_down)
    step = 512
    copies = 2 * -(-D // step) + -(-F // step)
    mixed, token_grad, weight_grad, gate_grad, up_grad, down_grad = pl.pallas_call(
        functools.partial(weight_kernel, (D, DP, CAP, step)),
        out_shape=returned
        + (
            jax.ShapeDtypeStruct((1, D, F), BF),
            jax.ShapeDtypeStruct((1, D, F), BF),
            jax.ShapeDtypeStruct((1, F, D), BF),
        ),
        in_specs=[anywhere] * 5 + [vmem] * 3,
        out_specs=[vmem] * 3 + [anywhere] * 3,
        scratch_shapes=[pltpu.VMEM(a.shape, a.dtype) for a in kept]
        + [
            pltpu.VMEM((D, F), BF),
            pltpu.VMEM((D, F), BF),
            pltpu.VMEM((F, D), BF),
            dma((5,)),
            dma((copies,)),
        ],
        compiler_params=pltpu.CompilerParams(vmem_limit_bytes=60 * 1024 * 1024),
        cost_estimate=pl.CostEstimate(
            flops=6 * 2 * CAP * D * F, bytes_accessed=6 * D * F, transcendentals=0
        ),
        name="weight_grads",
    )(*results[3:], *results[:3])
    return mixed, token_grad, jnp.swapaxes(weight_grad, 1, 2), gate_grad, up_grad, down_grad


def solution(mesh):
    pairs = P("rep", ("local", "strided"), None)
    split_last = P(("local", "strided"), None, "rep")
    split_middle = P(("local", "strided"), "rep", None)
    return jax.shard_map(
        local,
        mesh=mesh,
        in_specs=(pairs,) * 5 + (split_last, split_last, split_middle),
        out_specs=(pairs,) * 3 + (split_last, split_last, split_middle),
        check_vma=False,
    )
```

```python
import functools

import jax
import jax.numpy as jnp
from jax import lax
from jax.experimental import pallas as pl
from jax.experimental.pallas import tpu as pltpu
from jax.sharding import PartitionSpec as P

SWIGLU_ALPHA = 1.702
BF = jnp.bfloat16
F32 = jnp.float32
MESH = pl.DeviceIdType.MESH


def contract(left, right, left_dim, right_dim):
    return lax.dot_general(
        left, right, (((left_dim,), (right_dim,)), ((), ())), preferred_element_type=F32
    )


def xor(index, constant, size):
    result, bit = 0, 1
    while bit < size:
        result = result + bit * lax.rem(lax.div(index, bit) + (constant // bit) % 2, 2)
        bit *= 2
    return result


def three_parts(value):
    high = value.astype(BF).astype(F32)
    middle = (value - high).astype(BF).astype(F32)
    low = (value - high - middle).astype(BF).astype(F32)
    return high, middle, low


def kernel(
    sizes,
    tokens,
    experts,
    slots,
    router,
    out_grad,
    gate_hbm,
    up_hbm,
    down_hbm,
    mixed,
    token_grad,
    weight_grad,
    rows_hbm,
    grads_hbm,
    hidden_hbm,
    slope_gate_hbm,
    slope_up_hbm,
    w_gate,
    w_up,
    w_down,
    routing,
    gathered,
    plane_out,
    plane_in,
    back_out,
    back_in,
    home_out,
    home_in,
    select,
    place,
    rows,
    grads,
    hidden,
    gate_pre,
    up_pre,
    slope_gate,
    slope_up,
    partial,
    other,
    reply,
    w_sem,
    d_sem,
    z_send,
    z_recv,
    p_send,
    p_recv,
    r_send,
    r_recv,
    h_send,
    h_recv,
    c_send,
    c_recv,
):
    S, L, T, TOP, PM, G, R, D, DP, CAP = sizes
    NG, TT, LR = S // G, G * T, L * R
    TB = DP - 128
    OFF = D - TB
    l, s, r = lax.axis_index("local"), lax.axis_index("strided"), lax.axis_index("rep")
    twin = 1 - r
    strided_peers = [xor(s, j, S) for j in range(S)]
    local_peers = [xor(l, j, L) for j in range(L)]
    groups = [xor(lax.div(s, G), j, NG) for j in range(NG)]

    loads = [
        pltpu.make_async_copy(source.at[0], target, w_sem.at[i])
        for i, (source, target) in enumerate(
            ((gate_hbm, w_gate), (up_hbm, w_up), (down_hbm, w_down))
        )
    ]
    for load in loads:
        load.start()

    barrier = pltpu.get_barrier_semaphore()
    for j in range(1, S):
        pl.semaphore_signal(
            barrier, inc=1, device_id=(l, strided_peers[j], r), device_id_type=MESH
        )
    for j in range(1, L):
        pl.semaphore_signal(barrier, inc=1, device_id=(local_peers[j], s, r), device_id_type=MESH)
    pl.semaphore_signal(barrier, inc=1, device_id=(l, s, twin), device_id_type=MESH)

    lane = lax.broadcasted_iota(jnp.int32, (T, 128), 1) - OFF
    gathered[0, s, :, TB:] = jnp.zeros((T, 128), BF)
    gathered[1, s, :, TB:] = jnp.zeros((T, 128), BF)
    gathered[0, s, :, :D] = tokens[0]
    gathered[1, s, :, :D] = out_grad[0]
    routing[...] = jnp.zeros(routing.shape, F32)
    parts = (experts[0].astype(F32), slots[0].astype(F32) + 1.0) + three_parts(router[0])
    for i, part in enumerate(parts):
        routing[i * 16 : i * 16 + TOP, :] = part
    line = lax.broadcasted_iota(jnp.int32, (80, 128), 0)
    spot = lax.broadcasted_iota(jnp.int32, (80, 128), 1) - OFF
    spread = (lax.rem(line, 16) < TOP) & (spot == lax.div(line, 16) * TOP + lax.rem(line, 16))
    info = contract(routing[...].astype(BF), spread.astype(F32).astype(BF), 0, 0)
    tail = gathered[0, s, :, TB:].astype(F32)
    gathered[0, s, :, TB:] = jnp.where(lane < 0, tail, info).astype(BF)

    pl.semaphore_wait(barrier, (S - 1) + (L - 1) + 1)

    pending = []

    def send(source, target, send_sem, recv_sem, device):
        copy = pltpu.make_async_remote_copy(
            src_ref=source,
            dst_ref=target,
            send_sem=send_sem,
            recv_sem=recv_sem,
            device_id=device,
            device_id_type=MESH,
        )
        copy.start()
        pending.append(copy)
        return copy

    def arrival(target, send_sem, recv_sem, device):
        return pltpu.make_async_remote_copy(
            src_ref=target,
            dst_ref=target,
            send_sem=send_sem,
            recv_sem=recv_sem,
            device_id=device,
            device_id_type=MESH,
        )

    def send_strided(kind, j):
        send(
            gathered.at[kind, s],
            gathered.at[kind, s],
            z_send.at[kind, j],
            z_recv.at[kind, s],
            (l, strided_peers[j], r),
        )

    for j in range(1, S):
        send_strided(0, j)

    def await_strided(kind, buffer, sends, recvs, j):
        peer = strided_peers[j]
        arrival(
            buffer.at[kind, peer], sends.at[kind, j], recvs.at[kind, peer], (l, peer, r)
        ).wait_recv()

    def await_local(kind, buffer, sends, recvs, group, j):
        peer = local_peers[j]
        arrival(
            buffer.at[kind, group, peer],
            sends.at[kind, group, j],
            recvs.at[kind, group, peer],
            (peer, s, r),
        ).wait_recv()

    def send_local(kind, outgoing, incoming, sends, recvs, group):
        for j in range(1, L):
            send(
                outgoing.at[kind, group, local_peers[j]],
                incoming.at[kind, group, l],
                sends.at[kind, group, j],
                recvs.at[kind, group, l],
                (local_peers[j], s, r),
            )
        incoming[kind, group, l] = outgoing[kind, group, l]

    column = lax.broadcasted_iota(jnp.int32, (TT, LR), 1)
    token = lax.broadcasted_iota(jnp.int32, (TT, LR), 0)
    wanted = (lax.div(column, R) * S + s).astype(F32)
    same_source = lax.div(token, T) == lax.div(lax.rem(column, R), PM)
    rank_wanted = lax.rem(column, PM).astype(F32)
    below = (
        lax.broadcasted_iota(jnp.int32, (TT, TT), 1) < lax.broadcasted_iota(jnp.int32, (TT, TT), 0)
    ).astype(F32).astype(BF)
    group_lane = lax.broadcasted_iota(jnp.int32, (TT, 128), 1) - OFF
    row_lane = lax.broadcasted_iota(jnp.int32, (LR, 128), 1) - OFF

    for jg in range(NG):
        group = groups[jg]
        for j in range(max(1, jg * G), (jg + 1) * G):
            await_strided(0, gathered, z_send, z_recv, j)
            send_strided(1, j)
        block = gathered[0, pl.ds(group * G, G)].reshape(TT, DP)
        route = block[:, TB:].astype(F32)

        def lane_of(i, k):
            return route[:, OFF + i * TOP + k : OFF + i * TOP + k + 1]

        hits = []
        for k in range(TOP):
            hit = (lane_of(0, k) == wanted) & (lane_of(1, k) > 0.0) & same_source
            hits.append(hit.astype(F32))
        hit_any = sum(hits)
        rank = contract(below, hit_any.astype(BF), 1, 0)
        picked = jnp.where(rank == rank_wanted, hit_any, 0.0)
        picked_bf = picked.astype(BF)
        select[group] = picked_bf
        moved = contract(picked_bf, block, 0, 0)
        info = jnp.zeros((LR, 128), F32)
        for k in range(TOP):
            values = jnp.where(group_lane == 0, lane_of(1, k), 0.0)
            values = jnp.where(group_lane == 1, float(k), values)
            for i in range(3):
                values = jnp.where(group_lane == 2 + i, lane_of(2 + i, k), values)
            info = info + contract((picked * hits[k]).astype(BF), values.astype(BF), 0, 0)
        plane_out[0, group, :, :, :TB] = moved[:, :TB].astype(BF).reshape(L, R, TB)
        plane_out[0, group, :, :, TB:] = (
            jnp.where(row_lane < 0, moved[:, TB:], info).astype(BF).reshape(L, R, 128)
        )
        send_local(0, plane_out, plane_in, p_send, p_recv, group)

    for jg in range(NG):
        group = groups[jg]
        for j in range(max(1, jg * G), (jg + 1) * G):
            await_strided(1, gathered, z_send, z_recv, j)
        block = gathered[1, pl.ds(group * G, G)].reshape(TT, DP)
        moved = contract(select[group], block, 0, 0)
        plane_out[1, group] = moved.astype(BF).reshape(L, R, DP)
        send_local(1, plane_out, plane_in, p_send, p_recv, group)

    def swap(index, source, target):
        copy = send(source, target, c_send.at[index], c_recv.at[index], (l, s, twin))
        return copy

    def send_back(kind):
        for jg in reversed(range(NG)):
            group = groups[jg]
            spread_rows = contract(place[pl.ds(group * LR, LR), :], reply[kind], 1, 0)
            back_out[kind, group] = spread_rows.astype(BF).reshape(L, R, DP)
            send_local(kind, back_out, back_in, r_send, r_recv, group)

    middle = -(-D // 256) * 128
    halves = ((0, middle), (middle, D))

    def swap_half(kind, c):
        low, high = halves[c]
        index = 2 + 2 * kind + c
        swap(
            index,
            partial.at[kind, twin, :, pl.ds(low, high - low)],
            other.at[kind, :, pl.ds(low, high - low)],
        )

    def await_half(kind, c):
        low, high = halves[c]
        index = 2 + 2 * kind + c
        arrival(
            other.at[kind, :, pl.ds(low, high - low)],
            c_send.at[index],
            c_recv.at[index],
            (l, s, twin),
        ).wait_recv()

    saves = []

    def save(index, source, target):
        copy = pltpu.make_async_copy(source, target, d_sem.at[index])
        copy.start()
        saves.append(copy)

    def await_plane(kind):
        for jg in range(NG):
            for j in range(1, L):
                await_local(kind, plane_in, p_send, p_recv, groups[jg], j)

    await_plane(0)
    received = plane_in[0].reshape(NG * LR, DP)
    slot_of = received[:, TB:].astype(F32)[:, OFF : OFF + 1]
    slot_lane = lax.broadcasted_iota(jnp.int32, (NG * LR, CAP), 1).astype(F32) + 1.0
    place[...] = (slot_of == slot_lane).astype(F32).astype(BF)
    rows[0, r] = contract(place[...], received, 0, 0).astype(BF)
    swap(0, rows.at[0, r], rows.at[0, r])
    for load in loads:
        load.wait()
    arrival(rows.at[0, twin], c_send.at[0], c_recv.at[0], (l, s, twin)).wait_recv()

    x = rows[0].reshape(2 * CAP, DP)[:, :D]
    gate = contract(x, w_gate[...], 1, 0)
    gate_pre[...] = gate
    up = contract(x, w_up[...], 1, 0)
    up_pre[...] = up
    hidden[...] = ((up + 1.0) * gate * jax.nn.sigmoid(SWIGLU_ALPHA * gate)).astype(BF)
    save(2, hidden, hidden_hbm)
    save(0, rows.at[0], rows_hbm)
    for c, (low, high) in enumerate(halves):
        part = contract(hidden[...], w_down[:, low:high], 1, 0)
        partial[0, :, :, low:high] = part.reshape(2, CAP, high - low)
        swap_half(0, c)

    def weight_of(tail):
        return (
            tail[:, OFF + 2 : OFF + 3] + tail[:, OFF + 3 : OFF + 4] + tail[:, OFF + 4 : OFF + 5]
        )

    weight_rows = weight_of(rows[0].reshape(2 * CAP, DP)[:, TB:].astype(F32))
    own_tail = rows[0, r, :, TB:].astype(F32)
    await_half(0, 0)
    await_half(0, 1)
    out = partial[0, r] + other[0]
    reply[0, :, TB:] = jnp.zeros((CAP, 128), BF)
    reply[0, :, :D] = (weight_of(own_tail) * out).astype(BF)
    send_back(0)

    await_plane(1)
    rows[1, r] = contract(place[...], plane_in[1].reshape(NG * LR, DP), 0, 0).astype(BF)
    swap(1, rows.at[1, r], rows.at[1, r])
    own_grads = rows[1, r, :, :D].astype(F32)
    router_grad = jnp.sum(own_grads * out, axis=1, keepdims=True)
    slot_tail = lax.broadcasted_iota(jnp.int32, (CAP, 128), 1).astype(F32) - float(OFF)
    which = own_tail[:, OFF + 1 : OFF + 2]
    reply_tail = jnp.zeros((CAP, 128), F32)
    for i, part in enumerate(three_parts(router_grad)):
        reply_tail = jnp.where(slot_tail == which + float(i * TOP), part, reply_tail)
    arrival(rows.at[1, twin], c_send.at[1], c_recv.at[1], (l, s, twin)).wait_recv()
    grads[...] = (weight_rows * rows[1].reshape(2 * CAP, DP)[:, :D].astype(F32)).astype(BF)
    grad_hidden = contract(grads[...], w_down[...], 1, 1)
    gate = gate_pre[...]
    sig = jax.nn.sigmoid(SWIGLU_ALPHA * gate)
    slope_up[...] = (grad_hidden * gate * sig).astype(BF)
    slope = sig + SWIGLU_ALPHA * gate * sig * (1.0 - sig)
    slope_gate[...] = (grad_hidden * (up_pre[...] + 1.0) * slope).astype(BF)
    for c, (low, high) in enumerate(halves):
        part = contract(slope_gate[...], w_gate[low:high, :], 1, 1) + contract(
            slope_up[...], w_up[low:high, :], 1, 1
        )
        partial[1, :, :, low:high] = part.reshape(2, CAP, high - low)
        swap_half(1, c)
    save(1, grads, grads_hbm)
    save(3, slope_gate, slope_gate_hbm)
    save(4, slope_up, slope_up_hbm)
    await_half(1, 0)
    await_half(1, 1)
    reply[1, :, TB:] = jnp.zeros((CAP, 128), BF)
    reply[1, :, :D] = (partial[1, r] + other[1]).astype(BF)
    reply[1, :, TB:] = jnp.where(
        slot_tail < 0.0, reply[1, :, TB:].astype(F32), reply_tail
    ).astype(BF)
    send_back(1)

    def send_home(kind):
        for jg in reversed(range(NG)):
            group = groups[jg]
            for j in range(1, L):
                await_local(kind, back_in, r_send, r_recv, group, j)
            total = contract(select[group], back_in[kind, group].reshape(LR, DP), 1, 0)
            home_out[kind, pl.ds(group * G, G)] = total.astype(BF).reshape(G, T, DP)
            for j in range(jg * G, (jg + 1) * G):
                peer = strided_peers[j]
                if j == 0:
                    home_in[kind, s] = home_out[kind, s]
                else:
                    send(
                        home_out.at[kind, peer],
                        home_in.at[kind, s],
                        h_send.at[kind, j],
                        h_recv.at[kind, s],
                        (l, peer, r),
                    )

    send_home(0)
    send_home(1)

    def collect(kind):
        for j in range(1, S):
            await_strided(kind, home_in, h_send, h_recv, j)
        total = home_in[kind, 0].astype(F32)
        for j in range(1, S):
            total = total + home_in[kind, j].astype(F32)
        return total

    mixed[0] = collect(0)[:, :D].astype(BF)
    total = collect(1)
    token_grad[0] = total[:, :D].astype(BF)
    line = lax.broadcasted_iota(jnp.int32, (16, 128), 0)
    spot = lax.broadcasted_iota(jnp.int32, (16, 128), 1) - OFF
    chosen = (spot >= 0) & (spot < 3 * TOP) & (lax.rem(spot + 128, TOP) == line)
    weight_grad[0] = contract(
        chosen.astype(F32).astype(BF), total[:, TB:].astype(BF), 1, 1
    )[:TOP]
    for copy in saves:
        copy.wait()
    for copy in pending:
        copy.wait_send()


def weight_kernel(
    sizes,
    rows_hbm,
    grads_hbm,
    hidden_hbm,
    slope_gate_hbm,
    slope_up_hbm,
    mixed_in,
    token_grad_in,
    weight_grad_in,
    mixed,
    token_grad,
    weight_grad,
    gate_grad_hbm,
    up_grad_hbm,
    down_grad_hbm,
    rows,
    grads,
    hidden,
    slope_gate,
    slope_up,
    d_gate,
    d_up,
    d_down,
    in_sem,
    out_sem,
):
    D, DP, CAP, step = sizes
    F = hidden.shape[1]
    pairs = (
        (rows_hbm, rows),
        (slope_gate_hbm, slope_gate),
        (slope_up_hbm, slope_up),
        (grads_hbm, grads),
        (hidden_hbm, hidden),
    )
    loads = [
        pltpu.make_async_copy(source, target, in_sem.at[i])
        for i, (source, target) in enumerate(pairs)
    ]
    for load in loads:
        load.start()
    mixed[...] = mixed_in[...]
    token_grad[...] = token_grad_in[...]
    weight_grad[...] = weight_grad_in[...]
    stores = []

    def fill(left, right, target, out, limit):
        for low in range(0, limit, step):
            size = min(step, limit - low)
            target[low : low + size, :] = contract(
                left(low, low + size), right[...], 0, 0
            ).astype(BF)
            copy = pltpu.make_async_copy(
                target.at[pl.ds(low, size)],
                out.at[0, pl.ds(low, size)],
                out_sem.at[len(stores)],
            )
            copy.start()
            stores.append(copy)

    def row_columns(low, high):
        return rows[:, :, low:high].reshape(2 * CAP, high - low)

    loads[0].wait()
    loads[1].wait()
    fill(row_columns, slope_gate, d_gate, gate_grad_hbm, D)
    loads[2].wait()
    fill(row_columns, slope_up, d_up, up_grad_hbm, D)
    loads[3].wait()
    loads[4].wait()
    fill(lambda low, high: hidden[:, low:high], grads, d_down, down_grad_hbm, F)
    for copy in stores:
        copy.wait()


def local(tokens, experts, slots, route_weight, out_grad, w_gate, w_up, w_down):
    L, S = lax.axis_size("local"), lax.axis_size("strided")
    T, D = tokens.shape[1:]
    TOP = experts.shape[2]
    F = w_gate.shape[2]
    CAP = T * TOP
    PM = 2 * CAP // (L * S)
    G = max(1, 16 // PM)
    R = G * PM
    NG, TT, LR = S // G, G * T, L * R
    DP = -(-(D + 5 * TOP) // 128) * 128
    sizes = (S, L, T, TOP, PM, G, R, D, DP, CAP)
    vmem = pl.BlockSpec(memory_space=pltpu.VMEM)
    anywhere = pl.BlockSpec(memory_space=pl.ANY)
    dma = pltpu.SemaphoreType.DMA
    by_choice = [jnp.swapaxes(a, 1, 2) for a in (experts, slots, route_weight)]
    returned = (
        jax.ShapeDtypeStruct((1, T, D), BF),
        jax.ShapeDtypeStruct((1, T, D), BF),
        jax.ShapeDtypeStruct((1, TOP, T), F32),
    )
    kept = (
        jax.ShapeDtypeStruct((2, CAP, DP), BF),
        jax.ShapeDtypeStruct((2 * CAP, D), BF),
        jax.ShapeDtypeStruct((2 * CAP, F), BF),
        jax.ShapeDtypeStruct((2 * CAP, F), BF),
        jax.ShapeDtypeStruct((2 * CAP, F), BF),
    )
    results = pl.pallas_call(
        functools.partial(kernel, sizes),
        out_shape=returned + kept,
        in_specs=[vmem] * 5 + [anywhere] * 3,
        out_specs=[vmem] * 3 + [anywhere] * 5,
        scratch_shapes=[
            pltpu.VMEM((D, F), BF),
            pltpu.VMEM((D, F), BF),
            pltpu.VMEM((F, D), BF),
            pltpu.VMEM((80, T), F32),
            pltpu.VMEM((2, S, T, DP), BF),
            pltpu.VMEM((2, NG, L, R, DP), BF),
            pltpu.VMEM((2, NG, L, R, DP), BF),
            pltpu.VMEM((2, NG, L, R, DP), BF),
            pltpu.VMEM((2, NG, L, R, DP), BF),
            pltpu.VMEM((2, S, T, DP), BF),
            pltpu.VMEM((2, S, T, DP), BF),
            pltpu.VMEM((NG, TT, LR), BF),
            pltpu.VMEM((NG * LR, CAP), BF),
            pltpu.VMEM((2, 2, CAP, DP), BF),
            pltpu.VMEM((2 * CAP, D), BF),
            pltpu.VMEM((2 * CAP, F), BF),
            pltpu.VMEM((2 * CAP, F), F32),
            pltpu.VMEM((2 * CAP, F), F32),
            pltpu.VMEM((2 * CAP, F), BF),
            pltpu.VMEM((2 * CAP, F), BF),
            pltpu.VMEM((2, 2, CAP, D), F32),
            pltpu.VMEM((2, CAP, D), F32),
            pltpu.VMEM((2, CAP, DP), BF),
            dma((3,)),
            dma((5,)),
            dma((2, S)),
            dma((2, S)),
            dma((2, NG, L)),
            dma((2, NG, L)),
            dma((2, NG, L)),
            dma((2, NG, L)),
            dma((2, S)),
            dma((2, S)),
            dma((6,)),
            dma((6,)),
        ],
        compiler_params=pltpu.CompilerParams(
            collective_id=0, has_side_effects=True, vmem_limit_bytes=58 * 1024 * 1024
        ),
        cost_estimate=pl.CostEstimate(
            flops=12 * 2 * CAP * D * F, bytes_accessed=6 * D * F, transcendentals=4 * CAP * F
        ),
        name="moe_layer",
    )(tokens, *by_choice, out_grad, w_gate, w_up, w_down)
    step = 512
    copies = 2 * -(-D // step) + -(-F // step)
    mixed, token_grad, weight_grad, gate_grad, up_grad, down_grad = pl.pallas_call(
        functools.partial(weight_kernel, (D, DP, CAP, step)),
        out_shape=returned
        + (
            jax.ShapeDtypeStruct((1, D, F), BF),
            jax.ShapeDtypeStruct((1, D, F), BF),
            jax.ShapeDtypeStruct((1, F, D), BF),
        ),
        in_specs=[anywhere] * 5 + [vmem] * 3,
        out_specs=[vmem] * 3 + [anywhere] * 3,
        scratch_shapes=[pltpu.VMEM(a.shape, a.dtype) for a in kept]
        + [
            pltpu.VMEM((D, F), BF),
            pltpu.VMEM((D, F), BF),
            pltpu.VMEM((F, D), BF),
            dma((5,)),
            dma((copies,)),
        ],
        compiler_params=pltpu.CompilerParams(vmem_limit_bytes=60 * 1024 * 1024),
        cost_estimate=pl.CostEstimate(
            flops=6 * 2 * CAP * D * F, bytes_accessed=6 * D * F, transcendentals=0
        ),
        name="weight_grads",
    )(*results[3:], *results[:3])
    return mixed, token_grad, jnp.swapaxes(weight_grad, 1, 2), gate_grad, up_grad, down_grad


def solution(mesh):
    pairs = P("rep", ("local", "strided"), None)
    split_last = P(("local", "strided"), None, "rep")
    split_middle = P(("local", "strided"), "rep", None)
    return jax.shard_map(
        local,
        mesh=mesh,
        in_specs=(pairs,) * 5 + (split_last, split_last, split_middle),
        out_specs=(pairs,) * 3 + (split_last, split_last, split_middle),
        check_vma=False,
    )
```
